32 devices in a mesh: space: 8 (over z, y), mode: 4 (over x, core).
Axes of the slice: x: 2, y: 2, z: 4, core: 2. Of those that a mesh axis runs over, the one named last changes fastest.
Arguments:
- velocity: float32 [3, 128, 512, 256], P(None, 'space', 'mode'), may hold values from -6 to 6
- basis: float32 [32, 786432], P('mode', 'space'), may hold values from -42 to 42
- levels: float32 [8], replicated, may hold values from 0.02 to 0.15
- profile_index: int32 [256], replicated, may hold values from 0 to 7
- advect: float32 [256], replicated, may hold values from 0 to 0.4
Outputs:
- modes: float32 [32, 786432], P('mode', 'space')
- sigma: float32 [32], replicated
The draws below stay inside these ranges and needn't reach their ends.
Inputs may be any that keep to these rules, and one draw needn't show every extreme that they name: `profile_index`: each entry picks one of the 8 viscosity levels.
All inputs are finite; a program needn't handle non-finite values.
Results may differ from the reference program's by a relative error of at most 0.0055.
Values sent between devices are 32-bit elements; how exact they have to be, the bound alone decides.
A program may use at most 128 MiB of HBM per device.

```python
import math
import jax
import jax.numpy as jnp
import numpy as np
from jax import lax

CX = 16
CZ = 128
NY = 256
STRIDE = 4
MODES = 32
SWEEPS = 2
LEVELS = 8
NX = 128
NZ = 512
ROWS = 786432
N_SPACE = 8
N_MODE = 4


def draw_basis(key, part):
    key_noise = jax.random.fold_in(key, 11)
    key_rows = jax.random.fold_in(key, 12)
    key_cols = jax.random.fold_in(key, 13)
    noise = jnp.clip(jax.random.normal(key_noise, (MODES, ROWS), jnp.float32), -4.0, 4.0)
    mixed = noise + 0.4 * jnp.roll(noise, -1, axis=0)
    row_scale = jnp.exp(jax.random.uniform(key_rows, (1, ROWS), jnp.float32, math.log(0.25), math.log(2.5)))
    trend = 0.5 + jnp.arange(ROWS, dtype=jnp.float32)[None, :] / ROWS
    col_scale = jnp.exp(jax.random.uniform(key_cols, (MODES, 1), jnp.float32, math.log(0.5), math.log(2.0)))
    return mixed * row_scale * trend * col_scale


def touch_ends(entries, rng, smallest, top_value):
    dims = entries.shape
    index_at = [jax.random.randint(jax.random.fold_in(rng, axis), (), 0, dims[axis]) for axis in range(len(dims))]
    entries = entries.at[tuple(index_at)].set(smallest)
    longest = dims.index(max(dims))
    index_at[longest] = (index_at[longest] + 1) % dims[longest]
    return entries.at[tuple(index_at)].set(top_value)


def steps_of(key, dims, split, smallest, top_value):
    gain = 1.0
    for dim, blocks in split:
        draws = jax.random.uniform(jax.random.fold_in(jax.random.fold_in(key, 6), dim), (blocks,), jnp.float32, smallest / len(split), top_value / len(split))
        gain = gain * jnp.repeat(jnp.exp(draws), dims[dim] // blocks).reshape((-1,) + (1,) * (len(dims) - 1 - dim))
    return gain


def bell_draw(key, extent, deviation, reach, cuts=(), kind=jnp.bfloat16):
    drawn = deviation * jax.random.normal(key, extent, jnp.float32)
    if cuts:
        drawn = drawn * steps_of(key, extent, cuts, -0.22, 0.18)
    return jnp.clip(drawn, -reach, reach).astype(kind)


def setup_inputs(seed: int = 0) -> dict:
    arg_keys = jax.random.split(jax.random.key(seed), 6)
    velocity = bell_draw(arg_keys[0], (3, NX, NZ, NY), 1.0, 6.0, ((1, 8), (2, 4)), jnp.float32)
    basis = draw_basis(jax.random.fold_in(arg_keys[5], 71), 0)
    levels = jnp.clip(jnp.exp(jax.random.uniform(arg_keys[2], (LEVELS,), jnp.float32, math.log(0.02), math.log(0.15))), 0.02, 0.15)
    profile_index = touch_ends(jax.random.randint(arg_keys[3], (NY,), 0, LEVELS), jax.random.fold_in(arg_keys[3], 1), 0, LEVELS - 1).astype(jnp.int32)
    advect = jnp.clip(jax.random.uniform(arg_keys[4], (NY,), jnp.float32, 0.0, 0.4), 0.0, 0.4)
    return {"velocity": velocity, "basis": basis, "levels": levels, "profile_index": profile_index, "advect": advect}


def profile(levels, profile_index):
    table = (profile_index[:, None] == jnp.arange(levels.shape[0], dtype=jnp.int32)[None, :]).astype(jnp.float32)
    viscosity = lax.optimization_barrier(jnp.sum(table * levels[None, :], axis=1))
    middle = 0.5 * (viscosity[:-1] + viscosity[1:])
    face_up = jnp.concatenate([middle, viscosity[-1:]])
    face_down = jnp.concatenate([viscosity[:1], middle])
    return (viscosity, face_down, face_up)

def advance(field, viscosity, face_down, face_up, advect):
    center = field[:, 1:-1, 1:-1, :]
    east = field[:, 2:, 1:-1, :]
    west = field[:, :-2, 1:-1, :]
    north = field[:, 1:-1, 2:, :]
    south = field[:, 1:-1, :-2, :]
    walled = jnp.pad(center, ((0, 0), (0, 0), (0, 0), (1, 1)))
    upward = walled[..., 2:]
    downward = walled[..., :-2]
    lateral = east + west + north + south - 4.0 * center
    vertical = face_up * (upward - center) - face_down * (center - downward)
    return center + viscosity * lateral + vertical - 0.5 * advect * (east - west)

def box_sums(field):
    components, x_cells, z_cells, y_cells = field.shape
    boxes = field.reshape(components, x_cells // STRIDE, STRIDE, z_cells // STRIDE, STRIDE, y_cells // STRIDE, STRIDE)
    return lax.optimization_barrier(jnp.sum(boxes, axis=(2, 4, 6))) / math.sqrt(STRIDE ** 3)

def arrange(field):
    coarse = box_sums(field)
    blocks = coarse.reshape(3, N_SPACE, CX // STRIDE, N_MODE, CZ // STRIDE, NY // STRIDE)
    return blocks.transpose(1, 3, 0, 2, 4, 5).reshape(-1)

def pairing(count, turn):
    players = [0] + [1 + (i_pos - 1 + turn) % (count - 1) for i_pos in range(1, count)]
    leading = np.array(players[:count // 2])
    trailing = np.array([players[count - 1 - k_pos] for k_pos in range(count // 2)])
    return (leading, trailing)

def apply_pair(matrix, leading, trailing, cosine, sine_part):
    col_lead = matrix[:, leading]
    col_trail = matrix[:, trailing]
    matrix = matrix.at[:, leading].set(cosine * col_lead - sine_part * col_trail)
    return matrix.at[:, trailing].set(sine_part * col_lead + cosine * col_trail)

def jacobi_sweep(state):
    rotated, right_vecs = state
    count = rotated.shape[1]
    for turn in range(count - 1):
        leading, trailing = pairing(count, turn)
        col_lead = rotated[:, leading]
        col_trail = rotated[:, trailing]
        norm_lead = lax.optimization_barrier(jnp.sum(col_lead * col_lead, axis=0))
        norm_trail = lax.optimization_barrier(jnp.sum(col_trail * col_trail, axis=0))
        inner = lax.optimization_barrier(jnp.sum(col_lead * col_trail, axis=0))
        contrast = norm_trail - norm_lead
        orient = jnp.where(contrast >= 0.0, 1.0, -1.0)
        denominator = jnp.abs(contrast) + jnp.sqrt(contrast * contrast + 4.0 * inner * inner)
        positive = denominator > 0.0
        tangent = jnp.where(positive, 2.0 * inner * orient / jnp.where(positive, denominator, 1.0), 0.0)
        cosine = 1.0 / jnp.sqrt(1.0 + tangent * tangent)
        sine_part = cosine * tangent
        rotated = apply_pair(rotated, leading, trailing, cosine, sine_part)
        right_vecs = apply_pair(right_vecs, leading, trailing, cosine, sine_part)
    return (rotated, right_vecs)

def jacobi(upper):
    count = upper.shape[1]
    start = (upper, jnp.eye(count, dtype=jnp.float32))
    return lax.fori_loop(0, SWEEPS, lambda sweep_index, state: jacobi_sweep(state), start)

def reference(velocity, basis, levels, profile_index, advect):
    viscosity, face_down, face_up = profile(levels, profile_index)
    wrapped = jnp.pad(velocity, ((0, 0), (1, 1), (1, 1), (0, 0)), mode='wrap')
    first = advance(wrapped, viscosity, face_down, face_up, advect)
    wrapped = jnp.pad(first, ((0, 0), (1, 1), (1, 1), (0, 0)), mode='wrap')
    second = advance(wrapped, viscosity, face_down, face_up, advect)
    stack = jnp.concatenate([arrange(first)[None, :], arrange(second)[None, :], basis], axis=0)
    gram = lax.dot_general(stack.astype(jnp.float32), stack.astype(jnp.float32), (((1,), (1,)), ((), ())), precision=lax.Precision.HIGHEST, preferred_element_type=jnp.float32)
    lower = jnp.linalg.cholesky(gram)
    rotated, right_vecs = jacobi(lower.T)
    modes = jnp.dot(right_vecs[:, :MODES].T.astype(jnp.float32), stack.astype(jnp.float32), precision=lax.Precision.HIGHEST, preferred_element_type=jnp.float32)
    kept = rotated[:, :MODES]
    sigma = jnp.sqrt(lax.optimization_barrier(jnp.sum(kept * kept, axis=0)))
    return (modes, sigma)
```

```python
import functools
import math

import jax
import jax.numpy as jnp
import numpy as np
from jax import lax
from jax.experimental import pallas as pl
from jax.experimental.pallas import tpu as pltpu
from jax.sharding import PartitionSpec as P

STRIDE = 4
MODES = 32
SWEEPS = 2
COUNT = MODES + 2
HALF = COUNT // 2
ZB = 48
F32 = jnp.float32
BF16 = jnp.bfloat16
HIGH = lax.Precision.HIGHEST


def box_taps():
    lap = np.array([1.0, -2.0, 1.0])
    grad = np.array([-1.0, 0.0, 1.0])
    fixed = []
    for ops in ([], [lap], [grad], [lap, lap], [lap, grad], [grad, grad]):
        taps = np.zeros(STRIDE + 4)
        for x in range(STRIDE):
            terms = {x + 2: 1.0}
            for op in ops:
                nxt = {}
                for pos, val in terms.items():
                    for off, w in zip((-1, 0, 1), op):
                        if w:
                            nxt[pos + off] = nxt.get(pos + off, 0.0) + val * w
                terms = nxt
            for pos, val in terms.items():
                taps[pos] += val
        fixed.append(taps)
    return fixed


def z_table(cz):
    taps = box_taps()
    boxes = cz // STRIDE
    order = list(range(0, boxes, 2)) + list(range(1, boxes, 2)) + [-1, boxes]
    table = np.zeros((3 * ZB, 2 * cz), np.float32)
    for block, which in enumerate((0, 1, 3)):
        for row, box in enumerate(order):
            for k in range(STRIDE + 4):
                z = box * STRIDE - 2 + k
                if 0 <= z < cz:
                    table[block * ZB + row, z] = taps[which][k]
                    table[block * ZB + row, cz + z] = taps[which][k]
    return table


def column(row, width):
    size = row.shape[1]
    eye = lax.broadcasted_iota(jnp.int32, (size, size), 0) == lax.broadcasted_iota(
        jnp.int32, (size, size), 1
    )
    diag = jnp.where(eye, jnp.broadcast_to(row, (size, size)), 0.0)
    return jnp.dot(diag, jnp.ones((size, width), F32), precision=HIGH, preferred_element_type=F32)


def split(x):
    high = x.astype(BF16)
    return high, (x - high.astype(F32)).astype(BF16)


def wall_tables(levels_ref, index_ref, advect_ref, yh_ref, yl_ref):
    ny = index_ref.shape[1]
    nb = ny // STRIDE
    width = 2 * nb
    index = index_ref[...]
    nu_row = jnp.zeros((1, ny), F32)
    for level in range(levels_ref.shape[0]):
        nu_row = jnp.where(index == level, levels_ref[level], nu_row)
    nu = column(nu_row, width)
    adv = 0.5 * column(advect_ref[...], width)
    rows = lax.broadcasted_iota(jnp.int32, (ny, width), 0)
    lanes = lax.broadcasted_iota(jnp.int32, (ny, width), 1)
    below = lambda x: pltpu.roll(x, 1, 0)
    above = lambda x: pltpu.roll(x, ny - 1, 0)
    up = jnp.where(rows == ny - 1, nu, 0.5 * (nu + above(nu)))
    down = jnp.where(rows == 0, nu, 0.5 * (below(nu) + nu))
    main = 1.0 - up - down
    from_below = jnp.where(rows == 0, 0.0, below(up))
    from_above = jnp.where(rows == ny - 1, 0.0, above(down))

    def wall(x):
        return main * x + from_below * below(x) + from_above * above(x)

    box = jnp.where(lanes < nb, lanes, lanes - nb)
    x = jnp.where(rows // STRIDE == box, 1.0 / math.sqrt(STRIDE**3), 0.0)
    one = lanes < nb
    mx = wall(x)
    parts = [
        jnp.where(one, mx, wall(mx)),
        jnp.where(one, nu * x, nu * mx + wall(nu * x)),
        -jnp.where(one, adv * x, adv * mx + wall(adv * x)),
        jnp.where(one, 0.0, nu * nu * x),
        jnp.where(one, 0.0, -2.0 * nu * adv * x),
        jnp.where(one, 0.0, adv * adv * x),
    ]
    for k, part in enumerate(parts):
        high, low = split(part)
        yh_ref[k * ny : (k + 1) * ny, :] = high
        yl_ref[k * ny : (k + 1) * ny, :] = low


def coarse_box(v_ref, z_ref, yh_ref, yl_ref, f_ref, u_ref, c, jj):
    cx, cz, ny = v_ref.shape[1:]
    taps = box_taps()
    start = (jj - 1) * STRIDE - 2
    zc = 16

    def body(i, carry):
        at = pl.multiple_of(i * zc, zc)
        slabs = {
            k: v_ref[c, start + k, pl.ds(at, zc), :]
            for k in range(STRIDE + 4)
            if 0 <= start + k < cx
        }
        for f, coefs in enumerate(taps):
            total = None
            groups = {}
            for k, slab in slabs.items():
                if coefs[k]:
                    groups.setdefault(abs(coefs[k]), []).append((coefs[k] > 0, slab))
            for size, members in groups.items():
                part = None
                for plus, slab in sorted(members, key=lambda m: not m[0]):
                    if part is None:
                        part = slab if plus else -slab
                    else:
                        part = part + slab if plus else part - slab
                part = part if size == 1 else part * size
                total = part if total is None else total + part
            if total is None:
                total = jnp.zeros((zc, ny), F32)
            high, low = split(total)
            f_ref[pl.ds(at, zc), f * ny : (f + 1) * ny] = high
            f_ref[pl.ds(pl.multiple_of(cz + at, zc), zc), f * ny : (f + 1) * ny] = low
        return carry

    lax.fori_loop(0, cz // zc, body, 0)
    z0 = z_ref[0:ZB, :]

    def along_z(z, f):
        return jnp.dot(z, f_ref[:, f * ny : (f + 1) * ny], preferred_element_type=F32)

    z012_f0 = along_z(z_ref[...], 0)
    z01_f1 = along_z(z_ref[0 : 2 * ZB, :], 1)
    z01_f2 = along_z(z_ref[0 : 2 * ZB, :], 2)
    fields = [
        z012_f0[0:ZB],
        z01_f1[0:ZB] + z012_f0[ZB : 2 * ZB],
        z01_f2[0:ZB],
        along_z(z0, 3) + 2.0 * z01_f1[ZB : 2 * ZB] + z012_f0[2 * ZB : 3 * ZB],
        along_z(z0, 4) + z01_f2[ZB : 2 * ZB],
        along_z(z0, 5),
    ]
    out = None
    for k, field in enumerate(fields):
        high, low = split(field)
        yh = yh_ref[k * ny : (k + 1) * ny, :]
        yl = yl_ref[k * ny : (k + 1) * ny, :]
        both = jnp.dot(jnp.concatenate([high, low], axis=0), yh, preferred_element_type=F32)
        term = both[:ZB] + both[ZB:] + jnp.dot(high, yl, preferred_element_type=F32)
        out = term if out is None else out + term
    u_ref[jj, c, :, :] = out


def placed(rows, trail):
    row = lax.broadcasted_iota(jnp.int32, (rows, 128), 0)
    lane = lax.broadcasted_iota(jnp.int32, (rows, 128), 1)
    player = COUNT - 1 - lane if trail else lane
    where = jnp.where(player < 2, player, player + 6)
    return jnp.where((lane < HALF) & (row == where), 1.0, 0.0).astype(F32)


def jacobi(gram):
    rows = gram.shape[0]
    lead_v, trail_v = placed(rows, False), placed(rows, True)
    square = gram[:, :rows]
    lead_w = jnp.dot(square, lead_v, precision=HIGH, preferred_element_type=F32)
    trail_w = jnp.dot(square, trail_v, precision=HIGH, preferred_element_type=F32)
    lane = lax.broadcasted_iota(jnp.int32, (rows, 128), 1)
    first, last = lane == 0, lane == HALF - 1

    def turn(_, state):
        lw, lv, tw, tv = state
        a = jnp.sum(lw * lv, axis=0, keepdims=True)
        b = jnp.sum(tw * tv, axis=0, keepdims=True)
        c = jnp.sum(lv * tw, axis=0, keepdims=True)
        contrast = b - a
        orient = jnp.where(contrast >= 0.0, 2.0, -2.0)
        denominator = jnp.abs(contrast) + jnp.sqrt(contrast * contrast + 4.0 * c * c)
        positive = denominator > 0.0
        tangent = jnp.where(positive, c * orient / jnp.where(positive, denominator, 1.0), 0.0)
        cosine = lax.rsqrt(1.0 + tangent * tangent)
        sine = cosine * tangent

        def move(lead, trail):
            new_lead = cosine * lead - sine * trail
            new_trail = sine * lead + cosine * trail
            shifted = pltpu.roll(new_lead, 127, 1)
            next_lead = jnp.where(first, new_lead, jnp.where(last, new_trail, shifted))
            next_trail = jnp.where(first, shifted, pltpu.roll(new_trail, 1, 1))
            return next_lead, next_trail

        lw, tw = move(lw, tw)
        lv, tv = move(lv, tv)
        return lw, lv, tw, tv

    lw, lv, tw, tv = lax.fori_loop(
        0, SWEEPS * (COUNT - 1), turn, (lead_w, lead_v, trail_w, trail_v)
    )
    norm_lead = jnp.sum(lw * lv, axis=0, keepdims=True)
    norm_trail = jnp.sum(tw * tv, axis=0, keepdims=True)
    return lv, tv, norm_lead, norm_trail


def kernel(
    n_space, n_mode,
    velocity_ref, basis_ref, levels_ref, index_ref, advect_ref, z_ref,
    out_ref, sigma_ref,
    v_ref, stack_ref, yh_ref, yl_ref, f_ref, u_ref, xr_ref, zs_ref, zr_ref, sn_ref, row_ref,
    gram_ref, gm_ref, gs_ref,
    v_sem, own_sem,
    s1_send, s1_recv, mate_send, mate_recv, s2_send, s2_recv, fb_send, fb_recv, fa_send, fa_recv,
    x_send, x_recv, z_send, z_recv, sn_send, sn_recv, gm_send, gm_recv, gs_send, gs_recv,
):
    space, mode = lax.axis_index("space"), lax.axis_index("mode")
    mb, cols = basis_ref.shape
    quarter = cols // n_mode
    components, cx, cz, ny = velocity_ref.shape
    nxb, nzb, nb = cx // STRIDE, cz // STRIDE, ny // STRIDE
    pairs = n_mode // 2
    pair, side = mode // 2, mode % 2
    mate = pair * 2 + 1 - side
    MESH = pl.DeviceIdType.MESH

    def mode_peer(o):
        return lax.rem(mode + o, n_mode)

    def space_peer(o):
        return lax.rem(space + o, n_space)

    def rows_of(m):
        return pl.ds(pl.multiple_of(m * mb, mb), mb)

    def cols_of(q, count=1):
        return pl.ds(pl.multiple_of(q * quarter, quarter), count * quarter)

    def remote(src, dst, send, recv, s, m):
        return pltpu.make_async_remote_copy(
            src_ref=src, dst_ref=dst, send_sem=send, recv_sem=recv,
            device_id=(s, m), device_id_type=MESH,
        )

    v_copies = []
    for c in range(components):
        copy = pltpu.make_async_copy(velocity_ref.at[c], v_ref.at[c], v_sem.at[c])
        copy.start()
        v_copies.append(copy)
    own = pltpu.make_async_copy(basis_ref, stack_ref.at[rows_of(mode)], own_sem)
    own.start()

    barrier = pltpu.get_barrier_semaphore()
    for o in range(1, n_mode):
        pl.semaphore_signal(barrier, inc=1, device_id=(space, mode_peer(o)), device_id_type=MESH)
    for o in range(1, n_space):
        pl.semaphore_signal(barrier, inc=1, device_id=(space_peer(o), mode), device_id_type=MESH)
    pl.semaphore_wait(barrier, n_mode - 1 + n_space - 1)

    stage1 = []
    for o in range(1, n_mode):
        peer = mode_peer(o)
        copy = remote(
            basis_ref.at[:, cols_of(peer)], stack_ref.at[rows_of(mode), cols_of(peer)],
            s1_send.at[o - 1], s1_recv.at[o - 1], space, peer,
        )
        copy.start()
        stage1.append(copy)
    mates = []
    mate_cols = [cols_of(mode)] + [
        cols_of(2 * lax.rem(pair + g, pairs), 2) for g in range(1, pairs)
    ]
    for i, where in enumerate(mate_cols):
        copy = remote(
            basis_ref.at[:, where], stack_ref.at[rows_of(mode), where],
            mate_send.at[i], mate_recv.at[i], space, mate,
        )
        copy.start()
        mates.append(copy)

    wall_tables(levels_ref, index_ref, advect_ref, yh_ref, yl_ref)
    row_ref[...] = jnp.zeros_like(row_ref)
    zs_ref[...] = jnp.zeros_like(zs_ref)
    for copy in v_copies:
        copy.wait()

    def boxes(jj):
        def body(c, carry):
            coarse_box(v_ref, z_ref, yh_ref, yl_ref, f_ref, u_ref, c, jj)
            return carry

        lax.fori_loop(0, components, body, 0)

    boxes(0)
    boxes(nxb + 1)
    x_copies = [
        remote(u_ref.at[0], xr_ref.at[0], x_send.at[0], x_recv.at[0], space_peer(n_space - 1), mode),
        remote(u_ref.at[nxb + 1], xr_ref.at[1], x_send.at[1], x_recv.at[1], space_peer(1), mode),
    ]
    for copy in x_copies:
        copy.start()
    for jj in range(1, nxb + 1):
        boxes(jj)
    for copy in x_copies:
        copy.wait()
    for c in range(components):
        u_ref[nxb, c, :, :] = u_ref[nxb, c, :, :] + xr_ref[0, c, :, :]
        u_ref[1, c, :, :] = u_ref[1, c, :, :] + xr_ref[1, c, :, :]
    for c in range(components):
        for jj in range(1, nxb + 1):
            row = c * nxb + jj - 1
            for d in range(2):
                zs_ref[d, row : row + 1, :] = u_ref[jj, c, nzb + d : nzb + d + 1, :]
    z_copies = [
        remote(zs_ref.at[0], zr_ref.at[0], z_send.at[0], z_recv.at[0], space, mode_peer(n_mode - 1)),
        remote(zs_ref.at[1], zr_ref.at[1], z_send.at[1], z_recv.at[1], space, mode_peer(1)),
    ]
    for copy in z_copies:
        copy.start()
    for copy in z_copies:
        copy.wait()
    half = nzb // 2
    lanes = lax.broadcasted_iota(jnp.int32, (half, 2 * nb), 1) < nb
    for c in range(components):
        for jj in range(1, nxb + 1):
            row = c * nxb + jj - 1
            u_ref[jj, c, nzb - 1 : nzb, :] = u_ref[jj, c, nzb - 1 : nzb, :] + zr_ref[0, row : row + 1, :]
            u_ref[jj, c, 0:1, :] = u_ref[jj, c, 0:1, :] + zr_ref[1, row : row + 1, :]
            even = u_ref[jj, c, 0:half, :]
            odd = u_ref[jj, c, half:nzb, :]
            one = jnp.where(lanes, even, pltpu.roll(odd, nb, 1))
            two = jnp.where(lanes, pltpu.roll(even, nb, 1), odd)
            at = row * half
            sn_ref[mode, 0, at : at + half, :] = one
            sn_ref[mode, 1, at : at + half, :] = two
            for k in range(half):
                lane_at = (at + k) * 2 * nb
                row_ref[0:1, lane_at : lane_at + 2 * nb] = one[k : k + 1]
                row_ref[1:2, lane_at : lane_at + 2 * nb] = two[k : k + 1]
    sn_copies = []
    for o in range(1, n_mode):
        copy = remote(
            sn_ref.at[mode], sn_ref.at[mode], sn_send.at[o - 1], sn_recv.at[o - 1],
            space, mode_peer(o),
        )
        copy.start()
        sn_copies.append(copy)

    for copy in stage1:
        copy.wait()
    own.wait()
    forward_b = []
    for g in range(1, pairs):
        theirs = pl.ds(pl.multiple_of(2 * mb * lax.rem(pair + g, pairs), 2 * mb), 2 * mb)
        where = stack_ref.at[theirs, cols_of(mode)]
        copy = remote(where, where, fb_send.at[g - 1], fb_recv.at[g - 1], space, mate)
        copy.start()
        forward_b.append(copy)
    stage2 = []
    for g in range(1, pairs):
        for k in range(1, pairs):
            there = lax.rem(pair + g, pairs)
            piece = lax.rem(there + k, pairs)
            for part in range(2):
                i = ((g - 1) * (pairs - 1) + k - 1) * 2 + part
                where = cols_of(2 * piece + part)
                copy = remote(
                    basis_ref.at[:, where], stack_ref.at[rows_of(mode), where],
                    s2_send.at[i], s2_recv.at[i], space, 2 * there + side,
                )
                copy.start()
                source = lax.rem(pair - g + pairs, pairs)
                here = lax.rem(pair + k, pairs)
                stage2.append((copy, i, source, 2 * here + part))

    kc = 2048

    def gram_body(i, carry):
        at = pl.multiple_of(i * kc, kc)
        wide = pl.multiple_of(mode * quarter + i * kc, kc)
        x = jnp.concatenate([row_ref[:, pl.ds(at, kc)], stack_ref[:, pl.ds(wide, kc)]], axis=0)
        high, low = split(x)
        both = jnp.concatenate([high, low], axis=0)
        return carry + lax.dot_general(
            both, high, (((1,), (1,)), ((), ())), preferred_element_type=F32
        )

    size = 16 + stack_ref.shape[0]
    gram2 = lax.fori_loop(0, quarter // kc, gram_body, jnp.zeros((2 * size, size), F32))
    cross = gram2[size:]
    gram = gram2[:size] + cross + cross.T
    gram = jnp.concatenate([gram[0:8], gram[16:]], axis=0)
    gram = jnp.concatenate([gram[:, 0:8], gram[:, 16:], jnp.zeros((size - 8, 128 - size + 8), F32)], axis=1)
    gm_ref[mode, :, :] = gram
    gm_copies = []
    for o in range(1, n_mode):
        copy = remote(
            gm_ref.at[mode], gm_ref.at[mode], gm_send.at[o - 1], gm_recv.at[o - 1],
            space, mode_peer(o),
        )
        copy.start()
        gm_copies.append(copy)
    for copy in gm_copies:
        copy.wait()
    total = gm_ref[0]
    for m in range(1, n_mode):
        total = total + gm_ref[m]
    gs_ref[space, :, :] = total
    gs_copies = []
    for o in range(1, n_space):
        copy = remote(
            gs_ref.at[space], gs_ref.at[space], gs_send.at[o - 1], gs_recv.at[o - 1],
            space_peer(o), mode,
        )
        copy.start()
        gs_copies.append(copy)
    for copy in gs_copies:
        copy.wait()
    total = gs_ref[0]
    for s in range(1, n_space):
        total = total + gs_ref[s]

    lead, trail, norm_lead, norm_trail = jacobi(total)

    def pick(first, count, lead_side):
        row = lax.broadcasted_iota(jnp.int32, (count, 128), 0) + first
        lane = lax.broadcasted_iota(jnp.int32, (count, 128), 1)
        player = lane if lead_side else COUNT - 1 - lane
        return jnp.where((lane < HALF) & (row == player), 1.0, 0.0).astype(F32)

    def across(a, b):
        return lax.dot_general(
            a, b, (((1,), (1,)), ((), ())), precision=HIGH, preferred_element_type=F32
        )

    norms = across(jnp.broadcast_to(norm_lead, (8, 128)), pick(0, 128, True)) + across(
        jnp.broadcast_to(norm_trail, (8, 128)), pick(0, 128, False)
    )
    sigma_ref[...] = jnp.sqrt(norms)
    sel_lead, sel_trail = pick(mode * mb, mb, True), pick(mode * mb, mb, False)
    lead_b = jnp.concatenate([lead[8:], lead[8:]], axis=0)
    trail_b = jnp.concatenate([trail[8:], trail[8:]], axis=0)
    coef = across(sel_lead, lead_b) + across(sel_trail, trail_b)
    coef_high = coef.astype(BF16).astype(F32)
    left = jnp.concatenate([coef_high, coef - coef_high], axis=0).astype(BF16)
    snap = across(sel_lead, lead[0:8]) + across(sel_trail, trail[0:8])
    c0 = jnp.broadcast_to(snap[:, 0:1], (mb, 128))
    c1 = jnp.broadcast_to(snap[:, 1:2], (mb, 128))

    def emit(q):
        def body(i, carry):
            at = pl.multiple_of(q * quarter + i * kc, kc)
            high, low = split(stack_ref[:, pl.ds(at, kc)])
            both = jnp.concatenate([high, low], axis=0)
            done = jnp.dot(left, both, preferred_element_type=F32)
            done = done[:mb] + done[mb:]
            for t in range(kc // 128):
                r = i * (kc // 128) + t
                out_ref[:, pl.ds(pl.multiple_of(at + t * 128, 128), 128)] = (
                    done[:, t * 128 : (t + 1) * 128]
                    + c0 * sn_ref[q, 0, pl.ds(r, 1), :]
                    + c1 * sn_ref[q, 1, pl.ds(r, 1), :]
                )
            return carry

        lax.fori_loop(0, quarter // kc, body, 0)

    for copy in sn_copies + mates + forward_b:
        copy.wait()
    forward_a = []
    emit(2 * pair)
    for n, (copy, i, source, q) in enumerate(stage2):
        copy.wait()
        where = stack_ref.at[rows_of(2 * source + side), cols_of(q)]
        forward = remote(where, where, fa_send.at[i], fa_recv.at[i], space, mate)
        forward.start()
        forward_a.append(forward)
        if n == 0:
            emit(2 * pair + 1)
    if not stage2:
        emit(2 * pair + 1)
    for copy in forward_a:
        copy.wait()
    for o in range(2, n_mode):
        emit(lax.rem(2 * pair + o, n_mode))


def per_device(n_space, n_mode, velocity, basis, levels, profile_index, advect):
    components, cx, cz, ny = velocity.shape
    mb, cols = basis.shape
    quarter = cols // n_mode
    nxb, nzb, nb = cx // STRIDE, cz // STRIDE, ny // STRIDE
    pairs = n_mode // 2
    pieces = max(1, 2 * (pairs - 1) ** 2)
    dma = pltpu.SemaphoreType.DMA
    modes, sigma = pl.pallas_call(
        functools.partial(kernel, n_space, n_mode),
        out_shape=(
            jax.ShapeDtypeStruct((mb, cols), F32),
            jax.ShapeDtypeStruct((8, 128), F32),
        ),
        in_specs=[
            pl.BlockSpec(memory_space=pl.ANY),
            pl.BlockSpec(memory_space=pl.ANY),
            pl.BlockSpec(memory_space=pltpu.SMEM),
            pl.BlockSpec(memory_space=pltpu.VMEM),
            pl.BlockSpec(memory_space=pltpu.VMEM),
            pl.BlockSpec(memory_space=pltpu.VMEM),
        ],
        out_specs=(
            pl.BlockSpec(memory_space=pltpu.VMEM),
            pl.BlockSpec(memory_space=pltpu.VMEM),
        ),
        scratch_shapes=[
            pltpu.VMEM((components, cx, cz, ny), F32),
            pltpu.VMEM((n_mode * mb, cols), F32),
            pltpu.VMEM((6 * ny, 2 * nb), BF16),
            pltpu.VMEM((6 * ny, 2 * nb), BF16),
            pltpu.VMEM((2 * cz, 6 * ny), BF16),
            pltpu.VMEM((nxb + 2, components, ZB, 2 * nb), F32),
            pltpu.VMEM((2, components, ZB, 2 * nb), F32),
            pltpu.VMEM((2, 16, 2 * nb), F32),
            pltpu.VMEM((2, 16, 2 * nb), F32),
            pltpu.VMEM((n_mode, 2, components * nxb * nzb // 2, 2 * nb), F32),
            pltpu.VMEM((16, quarter), F32),
            pltpu.VMEM((8, 128), F32),
            pltpu.VMEM((n_mode, 8 + n_mode * mb, 128), F32),
            pltpu.VMEM((n_space, 8 + n_mode * mb, 128), F32),
            dma((components,)), dma,
            dma((n_mode - 1,)), dma((n_mode - 1,)),
            dma((pairs,)), dma((pairs,)),
            dma((pieces,)), dma((pieces,)),
            dma((max(1, pairs - 1),)), dma((max(1, pairs - 1),)),
            dma((pieces,)), dma((pieces,)),
            dma((2,)), dma((2,)),
            dma((2,)), dma((2,)),
            dma((n_mode - 1,)), dma((n_mode - 1,)),
            dma((n_mode - 1,)), dma((n_mode - 1,)),
            dma((n_space - 1,)), dma((n_space - 1,)),
        ],
        compiler_params=pltpu.CompilerParams(
            collective_id=0, has_side_effects=True, vmem_limit_bytes=56 * 1024 * 1024
        ),
    )(
        velocity,
        basis,
        levels,
        profile_index.reshape(1, -1),
        advect.reshape(1, -1),
        jnp.asarray(z_table(cz), BF16),
    )
    return modes, sigma[0, :MODES]


def solution(mesh):
    n_space, n_mode = mesh.shape["space"], mesh.shape["mode"]
    return jax.shard_map(
        functools.partial(per_device, n_space, n_mode),
        mesh=mesh,
        in_specs=(P(None, "space", "mode", None), P("mode", "space"), P(), P(), P()),
        out_specs=(P("mode", "space"), P()),
        check_vma=False,
    )
```

```python
import functools
import math

import jax
import jax.numpy as jnp
import numpy as np
from jax import lax
from jax.experimental import pallas as pl
from jax.experimental.pallas import tpu as pltpu
from jax.sharding import PartitionSpec as P

STRIDE = 4
MODES = 32
SWEEPS = 2
COUNT = MODES + 2
HALF = COUNT // 2
PIECES = 4
F32 = jnp.float32
BF16 = jnp.bfloat16
HIGH = lax.Precision.HIGHEST


def box_taps():
    lap = np.array([1.0, -2.0, 1.0])
    grad = np.array([-1.0, 0.0, 1.0])
    fixed = []
    for ops in ([], [lap], [grad], [lap, lap], [lap, grad], [grad, grad]):
        taps = np.zeros(STRIDE + 4)
        for x in range(STRIDE):
            terms = {x + 2: 1.0}
            for op in ops:
                nxt = {}
                for pos, val in terms.items():
                    for off, w in zip((-1, 0, 1), op):
                        if w:
                            nxt[pos + off] = nxt.get(pos + off, 0.0) + val * w
                terms = nxt
            for pos, val in terms.items():
                taps[pos] += val
        fixed.append(taps)
    return fixed


def z_table(cz):
    taps = box_taps()
    boxes = cz // STRIDE
    deep = cz + 16
    order = list(range(0, boxes, 2)) + list(range(1, boxes, 2))
    table = np.zeros((3 * boxes, 2 * deep), np.float32)
    for block, which in enumerate((0, 1, 3)):
        for row, box in enumerate(order):
            for k in range(STRIDE + 4):
                z = box * STRIDE - 2 + k
                at = cz + 10 + z if z < 0 else z
                table[block * boxes + row, at] = taps[which][k]
                table[block * boxes + row, deep + at] = taps[which][k]
    return table


def column(row, width):
    size = row.shape[1]
    eye = lax.broadcasted_iota(jnp.int32, (size, size), 0) == lax.broadcasted_iota(
        jnp.int32, (size, size), 1
    )
    diag = jnp.where(eye, jnp.broadcast_to(row, (size, size)), 0.0)
    return jnp.dot(diag, jnp.ones((size, width), F32), precision=HIGH, preferred_element_type=F32)


def split(x):
    high = x.astype(BF16)
    return high, (x - high.astype(F32)).astype(BF16)


def wall_tables(levels_ref, index_ref, advect_ref, yh_ref, yl_ref):
    ny = index_ref.shape[1]
    nb = ny // STRIDE
    width = 2 * nb
    index = index_ref[...]
    nu_row = jnp.zeros((1, ny), F32)
    for level in range(levels_ref.shape[0]):
        nu_row = jnp.where(index == level, levels_ref[level], nu_row)
    nu = column(nu_row, width)
    adv = 0.5 * column(advect_ref[...], width)
    rows = lax.broadcasted_iota(jnp.int32, (ny, width), 0)
    lanes = lax.broadcasted_iota(jnp.int32, (ny, width), 1)
    below = lambda x: pltpu.roll(x, 1, 0)
    above = lambda x: pltpu.roll(x, ny - 1, 0)
    up = jnp.where(rows == ny - 1, nu, 0.5 * (nu + above(nu)))
    down = jnp.where(rows == 0, nu, 0.5 * (below(nu) + nu))
    main = 1.0 - up - down
    from_below = jnp.where(rows == 0, 0.0, below(up))
    from_above = jnp.where(rows == ny - 1, 0.0, above(down))

    def wall(x):
        return main * x + from_below * below(x) + from_above * above(x)

    box = jnp.where(lanes < nb, lanes, lanes - nb)
    x = jnp.where(rows // STRIDE == box, 1.0 / math.sqrt(STRIDE**3), 0.0)
    one = lanes < nb
    mx = wall(x)
    parts = [
        jnp.where(one, mx, wall(mx)),
        jnp.where(one, nu * x, nu * mx + wall(nu * x)),
        -jnp.where(one, adv * x, adv * mx + wall(adv * x)),
        jnp.where(one, 0.0, nu * nu * x),
        jnp.where(one, 0.0, -2.0 * nu * adv * x),
        jnp.where(one, 0.0, adv * adv * x),
    ]
    for k, part in enumerate(parts):
        high, low = split(part)
        yh_ref[k * ny : (k + 1) * ny, :] = high
        yl_ref[k * ny : (k + 1) * ny, :] = low


def coarse_box(v_ref, z_ref, yh_ref, yl_ref, f_ref, u_ref, c, jj):
    cx, cz, ny = v_ref.shape[1:]
    taps = box_taps()
    start = (jj - 1) * STRIDE - 2
    zc = 16
    zb = z_ref.shape[0] // 3

    def body(i, carry):
        at = pl.multiple_of(i * zc, zc)
        slabs = {
            k: v_ref[c, start + k, pl.ds(at, zc), :]
            for k in range(STRIDE + 4)
            if 0 <= start + k < cx
        }
        for f, coefs in enumerate(taps):
            total = None
            groups = {}
            for k, slab in slabs.items():
                if coefs[k]:
                    groups.setdefault(abs(coefs[k]), []).append((coefs[k] > 0, slab))
            for size, members in groups.items():
                part = None
                for plus, slab in sorted(members, key=lambda m: not m[0]):
                    if part is None:
                        part = slab if plus else -slab
                    else:
                        part = part + slab if plus else part - slab
                part = part if size == 1 else part * size
                total = part if total is None else total + part
            if total is None:
                total = jnp.zeros((zc, ny), F32)
            high, low = split(total)
            f_ref[pl.ds(at, zc), f * ny : (f + 1) * ny] = high
            f_ref[pl.ds(pl.multiple_of(cz + at, zc), zc), f * ny : (f + 1) * ny] = low
        return carry

    lax.fori_loop(0, cz // zc, body, 0)
    z0 = z_ref[0:zb, :]

    def along_z(z, f):
        return jnp.dot(z, f_ref[:, f * ny : (f + 1) * ny], preferred_element_type=F32)

    z012_f0 = along_z(z_ref[...], 0)
    z01_f1 = along_z(z_ref[0 : 2 * zb, :], 1)
    z01_f2 = along_z(z_ref[0 : 2 * zb, :], 2)
    fields = [
        z012_f0[0:zb],
        z01_f1[0:zb] + z012_f0[zb : 2 * zb],
        z01_f2[0:zb],
        along_z(z0, 3) + 2.0 * z01_f1[zb : 2 * zb] + z012_f0[2 * zb : 3 * zb],
        along_z(z0, 4) + z01_f2[zb : 2 * zb],
        along_z(z0, 5),
    ]
    out = None
    for k, field in enumerate(fields):
        high, low = split(field)
        yh = yh_ref[k * ny : (k + 1) * ny, :]
        yl = yl_ref[k * ny : (k + 1) * ny, :]
        both = jnp.dot(jnp.concatenate([high, low], axis=0), yh, preferred_element_type=F32)
        term = both[:zb] + both[zb:] + jnp.dot(high, yl, preferred_element_type=F32)
        out = term if out is None else out + term
    u_ref[jj, c, :, :] = out


def placed(rows, trail):
    row = lax.broadcasted_iota(jnp.int32, (rows, 128), 0)
    lane = lax.broadcasted_iota(jnp.int32, (rows, 128), 1)
    player = COUNT - 1 - lane if trail else lane
    where = jnp.where(player < 2, player, player + 6)
    return jnp.where((lane < HALF) & (row == where), 1.0, 0.0).astype(F32)


def jacobi(gram):
    rows = gram.shape[0]
    lead_v, trail_v = placed(rows, False), placed(rows, True)
    square = gram[:, :rows]
    lead_w = jnp.dot(square, lead_v, precision=HIGH, preferred_element_type=F32)
    trail_w = jnp.dot(square, trail_v, precision=HIGH, preferred_element_type=F32)
    lane = lax.broadcasted_iota(jnp.int32, (rows, 128), 1)
    first, last = lane == 0, lane == HALF - 1

    def turn(_, state):
        lw, lv, tw, tv = state
        a = jnp.sum(lw * lv, axis=0, keepdims=True)
        b = jnp.sum(tw * tv, axis=0, keepdims=True)
        c = jnp.sum(lv * tw, axis=0, keepdims=True)
        contrast = b - a
        orient = jnp.where(contrast >= 0.0, 2.0, -2.0)
        denominator = jnp.abs(contrast) + jnp.sqrt(contrast * contrast + 4.0 * c * c)
        positive = denominator > 0.0
        tangent = jnp.where(positive, c * orient / jnp.where(positive, denominator, 1.0), 0.0)
        cosine = lax.rsqrt(1.0 + tangent * tangent)
        sine = cosine * tangent

        def move(lead, trail):
            new_lead = cosine * lead - sine * trail
            new_trail = sine * lead + cosine * trail
            shifted = pltpu.roll(new_lead, 127, 1)
            next_lead = jnp.where(first, new_lead, jnp.where(last, new_trail, shifted))
            next_trail = jnp.where(first, shifted, pltpu.roll(new_trail, 1, 1))
            return next_lead, next_trail

        lw, tw = move(lw, tw)
        lv, tv = move(lv, tv)
        return lw, lv, tw, tv

    lw, lv, tw, tv = lax.fori_loop(
        0, SWEEPS * (COUNT - 1), turn, (lead_w, lead_v, trail_w, trail_v)
    )
    norm_lead = jnp.sum(lw * lv, axis=0, keepdims=True)
    norm_trail = jnp.sum(tw * tv, axis=0, keepdims=True)
    return lv, tv, norm_lead, norm_trail


def kernel(
    n_space, n_mode,
    velocity_ref, basis_ref, levels_ref, index_ref, advect_ref, z_ref,
    out_ref, sigma_ref,
    v_ref, stack_ref, yh_ref, yl_ref, f_ref, u_ref, xr_ref, zs_ref, zr_ref, sn_ref, row_ref,
    gm_ref, gs_ref,
    v_sem, own_sem,
    s1_send, s1_recv, mate_send, mate_recv, s2_send, s2_recv, fb_send, fb_recv, fa_send, fa_recv,
    x_send, x_recv, z_send, z_recv, sn_send, sn_recv, gm_send, gm_recv, gs_send, gs_recv,
):
    space, mode = lax.axis_index("space"), lax.axis_index("mode")
    mb, cols = basis_ref.shape
    quarter = cols // n_mode
    components, cx, cz, ny = velocity_ref.shape
    nxb, nzb, nb = cx // STRIDE, cz // STRIDE, ny // STRIDE
    pairs = n_mode // 2
    pair, side = mode // 2, mode % 2
    mate = pair * 2 + 1 - side
    MESH = pl.DeviceIdType.MESH

    def mode_peer(o):
        return lax.rem(mode + o, n_mode)

    def space_peer(o):
        return lax.rem(space + o, n_space)

    def rows_of(m):
        return pl.ds(pl.multiple_of(m * mb, mb), mb)

    def cols_of(q, count=1):
        return pl.ds(pl.multiple_of(q * quarter, quarter), count * quarter)

    def remote(src, dst, send, recv, s, m):
        return pltpu.make_async_remote_copy(
            src_ref=src, dst_ref=dst, send_sem=send, recv_sem=recv,
            device_id=(s, m), device_id_type=MESH,
        )

    v_copies = []
    for c in range(components):
        copy = pltpu.make_async_copy(
            velocity_ref.at[c], v_ref.at[c, :, pl.ds(0, cz), :], v_sem.at[c]
        )
        copy.start()
        v_copies.append(copy)
    own = pltpu.make_async_copy(basis_ref, stack_ref.at[rows_of(mode)], own_sem)
    own.start()

    barrier = pltpu.get_barrier_semaphore()
    for o in range(1, n_mode):
        pl.semaphore_signal(barrier, inc=1, device_id=(space, mode_peer(o)), device_id_type=MESH)
    for o in range(1, n_space):
        pl.semaphore_signal(barrier, inc=1, device_id=(space_peer(o), mode), device_id_type=MESH)
    pl.semaphore_wait(barrier, n_mode - 1 + n_space - 1)

    stage1 = []

    def send1(first, count, slot):
        for o in range(1, n_mode):
            peer = mode_peer(o)
            where = pl.ds(pl.multiple_of(peer * quarter + first, 128), count)
            copy = remote(
                basis_ref.at[:, where], stack_ref.at[rows_of(mode), where],
                s1_send.at[slot, o - 1], s1_recv.at[slot, o - 1], space, peer,
            )
            copy.start()
            stage1.append(copy)

    eighth = quarter // 8
    send1(0, eighth, 0)
    for c in range(components):
        v_copies[c].wait()
        for x in range(cx):
            row = (c * cx + x) * 2
            zs_ref[0, row : row + 2, :] = v_ref[c, x, 0:2, :]
            zs_ref[1, row : row + 2, :] = v_ref[c, x, cz - 2 : cz, :]
    z_copies = [
        remote(zs_ref.at[0], zr_ref.at[0], z_send.at[0], z_recv.at[0], space, mode_peer(n_mode - 1)),
        remote(zs_ref.at[1], zr_ref.at[1], z_send.at[1], z_recv.at[1], space, mode_peer(1)),
    ]
    for copy in z_copies:
        copy.start()
    send1(eighth, quarter - eighth, 1)
    mates = []
    mate_cols = [cols_of(mode)] + [
        cols_of(2 * lax.rem(pair + g, pairs), 2) for g in range(1, pairs)
    ]
    for i, where in enumerate(mate_cols):
        copy = remote(
            basis_ref.at[:, where], stack_ref.at[rows_of(mode), where],
            mate_send.at[i], mate_recv.at[i], space, mate,
        )
        copy.start()
        mates.append(copy)

    wall_tables(levels_ref, index_ref, advect_ref, yh_ref, yl_ref)
    row_ref[...] = jnp.zeros_like(row_ref)
    for copy in z_copies:
        copy.wait()
    v_ref[:, :, cz : cz + 16, :] = jnp.zeros((components, cx, 16, ny), F32)
    for c in range(components):
        for x in range(cx):
            row = (c * cx + x) * 2
            for d in range(2):
                v_ref[c, x, cz + 8 * d : cz + 8 * d + 2, :] = zr_ref[d, row : row + 2, :]

    def boxes(jj):
        def body(c, carry):
            coarse_box(v_ref, z_ref, yh_ref, yl_ref, f_ref, u_ref, c, jj)
            return carry

        lax.fori_loop(0, components, body, 0)

    boxes(0)
    boxes(nxb + 1)
    x_copies = [
        remote(u_ref.at[0], xr_ref.at[0], x_send.at[0], x_recv.at[0], space_peer(n_space - 1), mode),
        remote(u_ref.at[nxb + 1], xr_ref.at[1], x_send.at[1], x_recv.at[1], space_peer(1), mode),
    ]
    for copy in x_copies:
        copy.start()
    for jj in range(1, nxb + 1):
        boxes(jj)
    for copy in x_copies:
        copy.wait()
    for c in range(components):
        u_ref[nxb, c, :, :] = u_ref[nxb, c, :, :] + xr_ref[0, c, :, :]
        u_ref[1, c, :, :] = u_ref[1, c, :, :] + xr_ref[1, c, :, :]
    half = nzb // 2
    lanes = lax.broadcasted_iota(jnp.int32, (half, 2 * nb), 1) < nb
    for c in range(components):
        for jj in range(1, nxb + 1):
            row = c * nxb + jj - 1
            even = u_ref[jj, c, 0:half, :]
            odd = u_ref[jj, c, half:nzb, :]
            one = jnp.where(lanes, even, pltpu.roll(odd, nb, 1))
            two = jnp.where(lanes, pltpu.roll(even, nb, 1), odd)
            at = row * half
            sn_ref[mode, 0, at : at + half, :] = one
            sn_ref[mode, 1, at : at + half, :] = two
            for k in range(half):
                lane_at = (at + k) * 2 * nb
                row_ref[0:1, lane_at : lane_at + 2 * nb] = one[k : k + 1]
                row_ref[1:2, lane_at : lane_at + 2 * nb] = two[k : k + 1]
    sn_mate = remote(sn_ref.at[mode], sn_ref.at[mode], sn_send.at[0], sn_recv.at[0], space, mate)
    sn_mate.start()

    for copy in stage1:
        copy.wait()
    own.wait()
    forward_b = []
    for g in range(1, pairs):
        theirs = pl.ds(pl.multiple_of(2 * mb * lax.rem(pair + g, pairs), 2 * mb), 2 * mb)
        where = stack_ref.at[theirs, cols_of(mode)]
        copy = remote(where, where, fb_send.at[g - 1], fb_recv.at[g - 1], space, mate)
        copy.start()
        forward_b.append(copy)
    sn_copies = []
    for g in range(1, pairs):
        copy = remote(
            sn_ref.at[mode], sn_ref.at[mode], sn_send.at[g], sn_recv.at[g],
            space, 2 * lax.rem(pair + g, pairs) + side,
        )
        copy.start()
        source = 2 * lax.rem(pair - g + pairs, pairs) + side
        sn_copies.append((copy, source, g))

    kc = 2048

    def gram_body(i, carry):
        at = pl.multiple_of(i * kc, kc)
        wide = pl.multiple_of(mode * quarter + i * kc, kc)
        x = jnp.concatenate([row_ref[:, pl.ds(at, kc)], stack_ref[:, pl.ds(wide, kc)]], axis=0)
        high, low = split(x)
        both = jnp.concatenate([high, low], axis=0)
        return carry + lax.dot_general(
            both, high, (((1,), (1,)), ((), ())), preferred_element_type=F32
        )

    size = 16 + stack_ref.shape[0]
    gram2 = lax.fori_loop(0, quarter // kc, gram_body, jnp.zeros((2 * size, size), F32))
    cross = gram2[size:]
    gram = gram2[:size] + cross + cross.T
    gram = jnp.concatenate([gram[0:8], gram[16:]], axis=0)
    gram = jnp.concatenate([gram[:, 0:8], gram[:, 16:], jnp.zeros((size - 8, 128 - size + 8), F32)], axis=1)
    gm_ref[mode, :, :] = gram
    gm_copies = []
    for o in range(1, n_mode):
        copy = remote(
            gm_ref.at[mode], gm_ref.at[mode], gm_send.at[o - 1], gm_recv.at[o - 1],
            space, mode_peer(o),
        )
        copy.start()
        gm_copies.append(copy)
    for copy in gm_copies:
        copy.wait()
    stage2 = []
    piece_cols = quarter // PIECES
    for part in range(2 * PIECES):
        for g in range(1, pairs):
            for k in range(1, pairs):
                i = ((g - 1) * (pairs - 1) + k - 1) * 2 * PIECES + part
                there = lax.rem(pair + g, pairs)

                def piece(group):
                    first = 2 * quarter * lax.rem(group, pairs) + part * piece_cols
                    return pl.ds(pl.multiple_of(first, piece_cols), piece_cols)

                where = piece(there + k)
                copy = remote(
                    basis_ref.at[:, where], stack_ref.at[rows_of(mode), where],
                    s2_send.at[i], s2_recv.at[i], space, 2 * there + side,
                )
                copy.start()
                source = 2 * lax.rem(pair - g + pairs, pairs) + side
                stage2.append((copy, i, source, piece(pair + k), lax.rem(pair + k, pairs), part))
    total = gm_ref[0]
    for m in range(1, n_mode):
        total = total + gm_ref[m]
    gs_ref[space, :, :] = total
    gs_copies = []
    for o in range(1, n_space):
        copy = remote(
            gs_ref.at[space], gs_ref.at[space], gs_send.at[o - 1], gs_recv.at[o - 1],
            space_peer(o), mode,
        )
        copy.start()
        gs_copies.append(copy)
    for copy in gs_copies:
        copy.wait()
    total = gs_ref[0]
    for s in range(1, n_space):
        total = total + gs_ref[s]

    lead, trail, norm_lead, norm_trail = jacobi(total)

    def pick(first, count, lead_side):
        row = lax.broadcasted_iota(jnp.int32, (count, 128), 0) + first
        lane = lax.broadcasted_iota(jnp.int32, (count, 128), 1)
        player = lane if lead_side else COUNT - 1 - lane
        return jnp.where((lane < HALF) & (row == player), 1.0, 0.0).astype(F32)

    def across(a, b):
        return lax.dot_general(
            a, b, (((1,), (1,)), ((), ())), precision=HIGH, preferred_element_type=F32
        )

    norms = across(jnp.broadcast_to(norm_lead, (8, 128)), pick(0, 128, True)) + across(
        jnp.broadcast_to(norm_trail, (8, 128)), pick(0, 128, False)
    )
    sigma_ref[...] = jnp.sqrt(norms[0:1, 0:MODES])
    sel_lead, sel_trail = pick(mode * mb, mb, True), pick(mode * mb, mb, False)
    lead_b = jnp.concatenate([lead[8:], lead[8:]], axis=0)
    trail_b = jnp.concatenate([trail[8:], trail[8:]], axis=0)
    coef = across(sel_lead, lead_b) + across(sel_trail, trail_b)
    coef_high = coef.astype(BF16).astype(F32)
    left = jnp.concatenate([coef_high, coef - coef_high], axis=0).astype(BF16)
    snap = across(sel_lead, lead[0:8]) + across(sel_trail, trail[0:8])
    c0 = jnp.broadcast_to(snap[:, 0:1], (mb, 128))
    c1 = jnp.broadcast_to(snap[:, 1:2], (mb, 128))

    def emit(q, first, count):
        def body(i, carry):
            at = pl.multiple_of(q * quarter + first + i * kc, kc)
            high, low = split(stack_ref[:, pl.ds(at, kc)])
            both = jnp.concatenate([high, low], axis=0)
            done = jnp.dot(left, both, preferred_element_type=F32)
            done = done[:mb] + done[mb:]
            for t in range(kc // 128):
                r = first // 128 + i * (kc // 128) + t
                out_ref[:, pl.ds(pl.multiple_of(at + t * 128, 128), 128)] = (
                    done[:, t * 128 : (t + 1) * 128]
                    + c0 * sn_ref[q, 0, pl.ds(r, 1), :]
                    + c1 * sn_ref[q, 1, pl.ds(r, 1), :]
                )
            return carry

        lax.fori_loop(0, count // kc, body, 0)

    for copy in mates + forward_b + [sn_mate]:
        copy.wait()
    sn_forward = []
    for copy, source, g in sn_copies:
        copy.wait()
        i = pairs + g - 1
        forward = remote(sn_ref.at[source], sn_ref.at[source], sn_send.at[i], sn_recv.at[i], space, mate)
        forward.start()
        sn_forward.append(forward)
    emit(2 * pair, 0, quarter)
    emit(2 * pair + 1, 0, quarter)
    for forward in sn_forward:
        forward.wait()
    size = (pairs - 1) ** 2
    before = []
    for n in range(0, len(stage2), size or 1):
        group = stage2[n : n + size]
        forwards = []
        for copy, i, source, where, _, _ in group:
            copy.wait()
            rows = stack_ref.at[rows_of(source), where]
            forward = remote(rows, rows, fa_send.at[i], fa_recv.at[i], space, mate)
            forward.start()
            forwards.append(forward)
        finish(before, emit, pairs, piece_cols)
        before = list(zip(forwards, group))
    finish(before, emit, pairs, piece_cols)


def finish(before, emit, pairs, piece_cols):
    for forward, _ in before:
        forward.wait()
    for _, (_, _, _, _, group, part) in before[: pairs - 1]:
        first = part * piece_cols
        quarter = PIECES * piece_cols
        emit(2 * group + first // quarter, first % quarter, piece_cols)


def per_device(n_space, n_mode, velocity, basis, levels, profile_index, advect):
    components, cx, cz, ny = velocity.shape
    mb, cols = basis.shape
    quarter = cols // n_mode
    nxb, nzb, nb = cx // STRIDE, cz // STRIDE, ny // STRIDE
    pairs = n_mode // 2
    pieces = max(1, 2 * PIECES * (pairs - 1) ** 2)
    dma = pltpu.SemaphoreType.DMA
    modes, sigma = pl.pallas_call(
        functools.partial(kernel, n_space, n_mode),
        out_shape=(
            jax.ShapeDtypeStruct((mb, cols), F32),
            jax.ShapeDtypeStruct((1, MODES), F32),
        ),
        in_specs=[
            pl.BlockSpec(memory_space=pl.ANY),
            pl.BlockSpec(memory_space=pl.ANY),
            pl.BlockSpec(memory_space=pltpu.SMEM),
            pl.BlockSpec(memory_space=pltpu.VMEM),
            pl.BlockSpec(memory_space=pltpu.VMEM),
            pl.BlockSpec(memory_space=pltpu.VMEM),
        ],
        out_specs=(
            pl.BlockSpec(memory_space=pltpu.VMEM),
            pl.BlockSpec(memory_space=pltpu.VMEM),
        ),
        scratch_shapes=[
            pltpu.VMEM((components, cx, cz + 16, ny), F32),
            pltpu.VMEM((n_mode * mb, cols), F32),
            pltpu.VMEM((6 * ny, 2 * nb), BF16),
            pltpu.VMEM((6 * ny, 2 * nb), BF16),
            pltpu.VMEM((2 * cz + 32, 6 * ny), BF16),
            pltpu.VMEM((nxb + 2, components, nzb, 2 * nb), F32),
            pltpu.VMEM((2, components, nzb, 2 * nb), F32),
            pltpu.VMEM((2, components * cx * 2, ny), F32),
            pltpu.VMEM((2, components * cx * 2, ny), F32),
            pltpu.VMEM((n_mode, 2, components * nxb * nzb // 2, 2 * nb), F32),
            pltpu.VMEM((16, quarter), F32),
            pltpu.VMEM((n_mode, 8 + n_mode * mb, 128), F32),
            pltpu.VMEM((n_space, 8 + n_mode * mb, 128), F32),
            dma((components,)), dma,
            dma((2, n_mode - 1)), dma((2, n_mode - 1)),
            dma((pairs,)), dma((pairs,)),
            dma((pieces,)), dma((pieces,)),
            dma((max(1, pairs - 1),)), dma((max(1, pairs - 1),)),
            dma((pieces,)), dma((pieces,)),
            dma((2,)), dma((2,)),
            dma((2,)), dma((2,)),
            dma((2 * pairs - 1,)), dma((2 * pairs - 1,)),
            dma((n_mode - 1,)), dma((n_mode - 1,)),
            dma((n_space - 1,)), dma((n_space - 1,)),
        ],
        compiler_params=pltpu.CompilerParams(
            collective_id=0, has_side_effects=True, vmem_limit_bytes=56 * 1024 * 1024
        ),
    )(
        velocity,
        basis,
        levels,
        profile_index.reshape(1, -1),
        advect.reshape(1, -1),
        jnp.asarray(z_table(cz), BF16),
    )
    return modes, sigma.reshape(-1)


def solution(mesh):
    n_space, n_mode = mesh.shape["space"], mesh.shape["mode"]
    return jax.shard_map(
        functools.partial(per_device, n_space, n_mode),
        mesh=mesh,
        in_specs=(P(None, "space", "mode", None), P("mode", "space"), P(), P(), P()),
        out_specs=(P("mode", "space"), P()),
        check_vma=False,
    )
```

```python
import functools
import math

import jax
import jax.numpy as jnp
import numpy as np
from jax import lax
from jax.experimental import pallas as pl
from jax.experimental.pallas import tpu as pltpu
from jax.sharding import PartitionSpec as P

STRIDE = 4
MODES = 32
SWEEPS = 2
COUNT = MODES + 2
HALF = COUNT // 2
PIECES = 4
F32 = jnp.float32
BF16 = jnp.bfloat16
HIGH = lax.Precision.HIGHEST


def box_taps():
    lap = np.array([1.0, -2.0, 1.0])
    grad = np.array([-1.0, 0.0, 1.0])
    fixed = []
    for ops in ([], [lap], [grad], [lap, lap], [lap, grad], [grad, grad]):
        taps = np.zeros(STRIDE + 4)
        for x in range(STRIDE):
            terms = {x + 2: 1.0}
            for op in ops:
                nxt = {}
                for pos, val in terms.items():
                    for off, w in zip((-1, 0, 1), op):
                        if w:
                            nxt[pos + off] = nxt.get(pos + off, 0.0) + val * w
                terms = nxt
            for pos, val in terms.items():
                taps[pos] += val
        fixed.append(taps)
    return fixed


def z_table(cz):
    taps = box_taps()
    boxes = cz // STRIDE
    deep = cz + 16
    order = list(range(0, boxes, 2)) + list(range(1, boxes, 2))
    table = np.zeros((3 * boxes, 2 * deep), np.float32)
    for block, which in enumerate((0, 1, 3)):
        for row, box in enumerate(order):
            for k in range(STRIDE + 4):
                z = box * STRIDE - 2 + k
                at = cz + 10 + z if z < 0 else z
                table[block * boxes + row, at] = taps[which][k]
                table[block * boxes + row, deep + at] = taps[which][k]
    return table


def column(row, width):
    size = row.shape[1]
    eye = lax.broadcasted_iota(jnp.int32, (size, size), 0) == lax.broadcasted_iota(
        jnp.int32, (size, size), 1
    )
    diag = jnp.where(eye, jnp.broadcast_to(row, (size, size)), 0.0)
    return jnp.dot(diag, jnp.ones((size, width), F32), precision=HIGH, preferred_element_type=F32)


def split(x):
    high = x.astype(BF16)
    return high, (x - high.astype(F32)).astype(BF16)


def wall_tables(levels_ref, index_ref, advect_ref, yh_ref, yl_ref):
    ny = index_ref.shape[1]
    nb = ny // STRIDE
    width = 2 * nb
    index = index_ref[...]
    nu_row = jnp.zeros((1, ny), F32)
    for level in range(levels_ref.shape[0]):
        nu_row = jnp.where(index == level, levels_ref[level], nu_row)
    nu = column(nu_row, width)
    adv = 0.5 * column(advect_ref[...], width)
    rows = lax.broadcasted_iota(jnp.int32, (ny, width), 0)
    lanes = lax.broadcasted_iota(jnp.int32, (ny, width), 1)
    below = lambda x: pltpu.roll(x, 1, 0)
    above = lambda x: pltpu.roll(x, ny - 1, 0)
    up = jnp.where(rows == ny - 1, nu, 0.5 * (nu + above(nu)))
    down = jnp.where(rows == 0, nu, 0.5 * (below(nu) + nu))
    main = 1.0 - up - down
    from_below = jnp.where(rows == 0, 0.0, below(up))
    from_above = jnp.where(rows == ny - 1, 0.0, above(down))

    def wall(x):
        return main * x + from_below * below(x) + from_above * above(x)

    box = jnp.where(lanes < nb, lanes, lanes - nb)
    x = jnp.where(rows // STRIDE == box, 1.0 / math.sqrt(STRIDE**3), 0.0)
    one = lanes < nb
    mx = wall(x)
    parts = [
        jnp.where(one, mx, wall(mx)),
        jnp.where(one, nu * x, nu * mx + wall(nu * x)),
        -jnp.where(one, adv * x, adv * mx + wall(adv * x)),
        jnp.where(one, 0.0, nu * nu * x),
        jnp.where(one, 0.0, -2.0 * nu * adv * x),
        jnp.where(one, 0.0, adv * adv * x),
    ]
    for k, part in enumerate(parts):
        high, low = split(part)
        yh_ref[k * ny : (k + 1) * ny, :] = high
        yl_ref[k * ny : (k + 1) * ny, :] = low


def coarse_box(v_ref, z_ref, yh_ref, yl_ref, f_ref, u_ref, c, jj):
    cx, cz, ny = v_ref.shape[1:]
    taps = box_taps()
    start = (jj - 1) * STRIDE - 2
    zc = 16
    zb = z_ref.shape[0] // 3

    def body(i, carry):
        at = pl.multiple_of(i * zc, zc)
        slabs = {
            k: v_ref[c, start + k, pl.ds(at, zc), :]
            for k in range(STRIDE + 4)
            if 0 <= start + k < cx
        }
        for f, coefs in enumerate(taps):
            total = None
            groups = {}
            for k, slab in slabs.items():
                if coefs[k]:
                    groups.setdefault(abs(coefs[k]), []).append((coefs[k] > 0, slab))
            for size, members in groups.items():
                part = None
                for plus, slab in sorted(members, key=lambda m: not m[0]):
                    if part is None:
                        part = slab if plus else -slab
                    else:
                        part = part + slab if plus else part - slab
                part = part if size == 1 else part * size
                total = part if total is None else total + part
            if total is None:
                total = jnp.zeros((zc, ny), F32)
            high, low = split(total)
            f_ref[pl.ds(at, zc), f * ny : (f + 1) * ny] = high
            f_ref[pl.ds(pl.multiple_of(cz + at, zc), zc), f * ny : (f + 1) * ny] = low
        return carry

    lax.fori_loop(0, cz // zc, body, 0)
    z0 = z_ref[0:zb, :]

    def along_z(z, f):
        return jnp.dot(z, f_ref[:, f * ny : (f + 1) * ny], preferred_element_type=F32)

    z012_f0 = along_z(z_ref[...], 0)
    z01_f1 = along_z(z_ref[0 : 2 * zb, :], 1)
    z01_f2 = along_z(z_ref[0 : 2 * zb, :], 2)
    fields = [
        z012_f0[0:zb],
        z01_f1[0:zb] + z012_f0[zb : 2 * zb],
        z01_f2[0:zb],
        along_z(z0, 3) + 2.0 * z01_f1[zb : 2 * zb] + z012_f0[2 * zb : 3 * zb],
        along_z(z0, 4) + z01_f2[zb : 2 * zb],
        along_z(z0, 5),
    ]
    out = None
    for k, field in enumerate(fields):
        high, low = split(field)
        yh = yh_ref[k * ny : (k + 1) * ny, :]
        yl = yl_ref[k * ny : (k + 1) * ny, :]
        both = jnp.dot(jnp.concatenate([high, low], axis=0), yh, preferred_element_type=F32)
        term = both[:zb] + both[zb:] + jnp.dot(high, yl, preferred_element_type=F32)
        out = term if out is None else out + term
    u_ref[jj, c, :, :] = out


def placed(rows, trail):
    row = lax.broadcasted_iota(jnp.int32, (rows, 128), 0)
    lane = lax.broadcasted_iota(jnp.int32, (rows, 128), 1)
    player = COUNT - 1 - lane if trail else lane
    where = jnp.where(player < 2, player, player + 6)
    return jnp.where((lane < HALF) & (row == where), 1.0, 0.0).astype(F32)


def jacobi(gram):
    rows = gram.shape[0]
    lead_v, trail_v = placed(rows, False), placed(rows, True)
    square = gram[:, :rows]
    lead_w = jnp.dot(square, lead_v, precision=HIGH, preferred_element_type=F32)
    trail_w = jnp.dot(square, trail_v, precision=HIGH, preferred_element_type=F32)
    lane = lax.broadcasted_iota(jnp.int32, (rows, 128), 1)
    first, last = lane == 0, lane == HALF - 1

    def turn(_, state):
        lw, lv, tw, tv = state
        a = jnp.sum(lw * lv, axis=0, keepdims=True)
        b = jnp.sum(tw * tv, axis=0, keepdims=True)
        c = jnp.sum(lv * tw, axis=0, keepdims=True)
        contrast = b - a
        orient = jnp.where(contrast >= 0.0, 2.0, -2.0)
        denominator = jnp.abs(contrast) + jnp.sqrt(contrast * contrast + 4.0 * c * c)
        positive = denominator > 0.0
        tangent = jnp.where(positive, c * orient / jnp.where(positive, denominator, 1.0), 0.0)
        cosine = lax.rsqrt(1.0 + tangent * tangent)
        sine = cosine * tangent

        def move(lead, trail):
            new_lead = cosine * lead - sine * trail
            new_trail = sine * lead + cosine * trail
            shifted = pltpu.roll(new_lead, 127, 1)
            next_lead = jnp.where(first, new_lead, jnp.where(last, new_trail, shifted))
            next_trail = jnp.where(first, shifted, pltpu.roll(new_trail, 1, 1))
            return next_lead, next_trail

        lw, tw = move(lw, tw)
        lv, tv = move(lv, tv)
        return lw, lv, tw, tv

    lw, lv, tw, tv = lax.fori_loop(
        0, SWEEPS * (COUNT - 1), turn, (lead_w, lead_v, trail_w, trail_v)
    )
    norm_lead = jnp.sum(lw * lv, axis=0, keepdims=True)
    norm_trail = jnp.sum(tw * tv, axis=0, keepdims=True)
    return lv, tv, norm_lead, norm_trail


def kernel(
    n_space, n_mode,
    velocity_ref, basis_ref, levels_ref, index_ref, advect_ref, z_ref,
    modes_ref, sigma_ref,
    out_ref, v_ref, stack_ref, yh_ref, yl_ref, f_ref, u_ref, xr_ref, zs_ref, zr_ref, sn_ref, row_ref,
    gm_ref, gs_ref,
    v_sem, own_sem, out_sem,
    s1_send, s1_recv, mate_send, mate_recv, s2_send, s2_recv, fb_send, fb_recv, fa_send, fa_recv,
    x_send, x_recv, z_send, z_recv, sn_send, sn_recv, gm_send, gm_recv, gs_send, gs_recv,
):
    space, mode = lax.axis_index("space"), lax.axis_index("mode")
    mb, cols = basis_ref.shape
    quarter = cols // n_mode
    components, cx, cz, ny = velocity_ref.shape
    nxb, nzb, nb = cx // STRIDE, cz // STRIDE, ny // STRIDE
    pairs = n_mode // 2
    pair, side = mode // 2, mode % 2
    mate = pair * 2 + 1 - side
    MESH = pl.DeviceIdType.MESH

    def mode_peer(o):
        return lax.rem(mode + o, n_mode)

    def space_peer(o):
        return lax.rem(space + o, n_space)

    def rows_of(m):
        return pl.ds(pl.multiple_of(m * mb, mb), mb)

    def cols_of(q, count=1):
        return pl.ds(pl.multiple_of(q * quarter, quarter), count * quarter)

    def remote(src, dst, send, recv, s, m):
        return pltpu.make_async_remote_copy(
            src_ref=src, dst_ref=dst, send_sem=send, recv_sem=recv,
            device_id=(s, m), device_id_type=MESH,
        )

    v_copies = []
    for c in range(components):
        copy = pltpu.make_async_copy(
            velocity_ref.at[c], v_ref.at[c, :, pl.ds(0, cz), :], v_sem.at[c]
        )
        copy.start()
        v_copies.append(copy)
    own = pltpu.make_async_copy(basis_ref, stack_ref.at[rows_of(mode)], own_sem)
    own.start()

    barrier = pltpu.get_barrier_semaphore()
    for o in range(1, n_mode):
        pl.semaphore_signal(barrier, inc=1, device_id=(space, mode_peer(o)), device_id_type=MESH)
    for o in range(1, n_space):
        pl.semaphore_signal(barrier, inc=1, device_id=(space_peer(o), mode), device_id_type=MESH)
    pl.semaphore_wait(barrier, n_mode - 1 + n_space - 1)

    stage1 = []

    def send1(first, count, slot):
        for o in range(1, n_mode):
            peer = mode_peer(o)
            where = pl.ds(pl.multiple_of(peer * quarter + first, 128), count)
            copy = remote(
                basis_ref.at[:, where], stack_ref.at[rows_of(mode), where],
                s1_send.at[slot, o - 1], s1_recv.at[slot, o - 1], space, peer,
            )
            copy.start()
            stage1.append(copy)

    eighth = quarter // 8
    send1(0, eighth, 0)
    for c in range(components):
        v_copies[c].wait()
        for x in range(cx):
            row = (c * cx + x) * 2
            zs_ref[0, row : row + 2, :] = v_ref[c, x, 0:2, :]
            zs_ref[1, row : row + 2, :] = v_ref[c, x, cz - 2 : cz, :]
    z_copies = [
        remote(zs_ref.at[0], zr_ref.at[0], z_send.at[0], z_recv.at[0], space, mode_peer(n_mode - 1)),
        remote(zs_ref.at[1], zr_ref.at[1], z_send.at[1], z_recv.at[1], space, mode_peer(1)),
    ]
    for copy in z_copies:
        copy.start()
    send1(eighth, quarter - eighth, 1)
    mates = []
    mate_cols = [cols_of(mode)] + [
        cols_of(2 * lax.rem(pair + g, pairs), 2) for g in range(1, pairs)
    ]
    for i, where in enumerate(mate_cols):
        copy = remote(
            basis_ref.at[:, where], stack_ref.at[rows_of(mode), where],
            mate_send.at[i], mate_recv.at[i], space, mate,
        )
        copy.start()
        mates.append(copy)

    wall_tables(levels_ref, index_ref, advect_ref, yh_ref, yl_ref)
    row_ref[...] = jnp.zeros_like(row_ref)
    for copy in z_copies:
        copy.wait()
    v_ref[:, :, cz : cz + 16, :] = jnp.zeros((components, cx, 16, ny), F32)
    for c in range(components):
        for x in range(cx):
            row = (c * cx + x) * 2
            for d in range(2):
                v_ref[c, x, cz + 8 * d : cz + 8 * d + 2, :] = zr_ref[d, row : row + 2, :]

    def boxes(jj):
        def body(c, carry):
            coarse_box(v_ref, z_ref, yh_ref, yl_ref, f_ref, u_ref, c, jj)
            return carry

        lax.fori_loop(0, components, body, 0)

    boxes(0)
    boxes(nxb + 1)
    x_copies = [
        remote(u_ref.at[0], xr_ref.at[0], x_send.at[0], x_recv.at[0], space_peer(n_space - 1), mode),
        remote(u_ref.at[nxb + 1], xr_ref.at[1], x_send.at[1], x_recv.at[1], space_peer(1), mode),
    ]
    for copy in x_copies:
        copy.start()
    for jj in range(1, nxb + 1):
        boxes(jj)
    for copy in x_copies:
        copy.wait()
    for c in range(components):
        u_ref[nxb, c, :, :] = u_ref[nxb, c, :, :] + xr_ref[0, c, :, :]
        u_ref[1, c, :, :] = u_ref[1, c, :, :] + xr_ref[1, c, :, :]
    half = nzb // 2
    lanes = lax.broadcasted_iota(jnp.int32, (half, 2 * nb), 1) < nb
    for c in range(components):
        for jj in range(1, nxb + 1):
            row = c * nxb + jj - 1
            even = u_ref[jj, c, 0:half, :]
            odd = u_ref[jj, c, half:nzb, :]
            one = jnp.where(lanes, even, pltpu.roll(odd, nb, 1))
            two = jnp.where(lanes, pltpu.roll(even, nb, 1), odd)
            at = row * half
            sn_ref[mode, 0, at : at + half, :] = one
            sn_ref[mode, 1, at : at + half, :] = two
            for k in range(half):
                lane_at = (at + k) * 2 * nb
                row_ref[0:1, lane_at : lane_at + 2 * nb] = one[k : k + 1]
                row_ref[1:2, lane_at : lane_at + 2 * nb] = two[k : k + 1]
    sn_mate = remote(sn_ref.at[mode], sn_ref.at[mode], sn_send.at[0], sn_recv.at[0], space, mate)
    sn_mate.start()
    sn_copies = []
    for g in range(1, pairs):
        copy = remote(
            sn_ref.at[mode], sn_ref.at[mode], sn_send.at[g], sn_recv.at[g],
            space, 2 * lax.rem(pair + g, pairs) + side,
        )
        copy.start()
        source = 2 * lax.rem(pair - g + pairs, pairs) + side
        sn_copies.append((copy, source, g))

    for copy in stage1:
        copy.wait()
    own.wait()
    forward_b = []
    for g in range(1, pairs):
        theirs = pl.ds(pl.multiple_of(2 * mb * lax.rem(pair + g, pairs), 2 * mb), 2 * mb)
        where = stack_ref.at[theirs, cols_of(mode)]
        copy = remote(where, where, fb_send.at[g - 1], fb_recv.at[g - 1], space, mate)
        copy.start()
        forward_b.append(copy)
    stage2 = []
    piece_cols = quarter // PIECES

    def send2(part):
        for g in range(1, pairs):
            for k in range(1, pairs):
                i = ((g - 1) * (pairs - 1) + k - 1) * 2 * PIECES + part
                there = lax.rem(pair + g, pairs)

                def piece(group):
                    first = 2 * quarter * lax.rem(group, pairs) + part * piece_cols
                    return pl.ds(pl.multiple_of(first, piece_cols), piece_cols)

                where = piece(there + k)
                copy = remote(
                    basis_ref.at[:, where], stack_ref.at[rows_of(mode), where],
                    s2_send.at[i], s2_recv.at[i], space, 2 * there + side,
                )
                copy.start()
                source = 2 * lax.rem(pair - g + pairs, pairs) + side
                stage2.append((copy, i, source, piece(pair + k), lax.rem(pair + k, pairs), part))

    send2(0)
    kc = 2048

    def gram_body(i, carry):
        at = pl.multiple_of(i * kc, kc)
        wide = pl.multiple_of(mode * quarter + i * kc, kc)
        x = jnp.concatenate([row_ref[:, pl.ds(at, kc)], stack_ref[:, pl.ds(wide, kc)]], axis=0)
        high, low = split(x)
        both = jnp.concatenate([high, low], axis=0)
        return carry + lax.dot_general(
            both, high, (((1,), (1,)), ((), ())), preferred_element_type=F32
        )

    size = 16 + stack_ref.shape[0]
    gram2 = lax.fori_loop(0, quarter // kc, gram_body, jnp.zeros((2 * size, size), F32))
    cross = gram2[size:]
    gram = gram2[:size] + cross + cross.T
    gram = jnp.concatenate([gram[0:8], gram[16:]], axis=0)
    gram = jnp.concatenate([gram[:, 0:8], gram[:, 16:], jnp.zeros((size - 8, 128 - size + 8), F32)], axis=1)
    gm_ref[mode, :, :] = gram
    gm_copies = []
    for o in range(1, n_mode):
        copy = remote(
            gm_ref.at[mode], gm_ref.at[mode], gm_send.at[o - 1], gm_recv.at[o - 1],
            space, mode_peer(o),
        )
        copy.start()
        gm_copies.append(copy)
    send2(1)
    for copy in gm_copies:
        copy.wait()
    for part in range(2, 2 * PIECES):
        send2(part)
    total = gm_ref[0]
    for m in range(1, n_mode):
        total = total + gm_ref[m]
    gs_ref[space, :, :] = total
    gs_copies = []
    for o in range(1, n_space):
        copy = remote(
            gs_ref.at[space], gs_ref.at[space], gs_send.at[o - 1], gs_recv.at[o - 1],
            space_peer(o), mode,
        )
        copy.start()
        gs_copies.append(copy)
    for copy in gs_copies:
        copy.wait()
    total = gs_ref[0]
    for s in range(1, n_space):
        total = total + gs_ref[s]

    lead, trail, norm_lead, norm_trail = jacobi(total)

    def pick(first, count, lead_side):
        row = lax.broadcasted_iota(jnp.int32, (count, 128), 0) + first
        lane = lax.broadcasted_iota(jnp.int32, (count, 128), 1)
        player = lane if lead_side else COUNT - 1 - lane
        return jnp.where((lane < HALF) & (row == player), 1.0, 0.0).astype(F32)

    def across(a, b):
        return lax.dot_general(
            a, b, (((1,), (1,)), ((), ())), precision=HIGH, preferred_element_type=F32
        )

    norms = across(jnp.broadcast_to(norm_lead, (8, 128)), pick(0, 128, True)) + across(
        jnp.broadcast_to(norm_trail, (8, 128)), pick(0, 128, False)
    )
    sigma_ref[...] = jnp.sqrt(norms[0:1, 0:MODES])
    sel_lead, sel_trail = pick(mode * mb, mb, True), pick(mode * mb, mb, False)
    lead_b = jnp.concatenate([lead[8:], lead[8:]], axis=0)
    trail_b = jnp.concatenate([trail[8:], trail[8:]], axis=0)
    coef = across(sel_lead, lead_b) + across(sel_trail, trail_b)
    coef_high = coef.astype(BF16).astype(F32)
    left = jnp.concatenate([coef_high, coef - coef_high], axis=0).astype(BF16)
    snap = across(sel_lead, lead[0:8]) + across(sel_trail, trail[0:8])
    c0 = jnp.broadcast_to(snap[:, 0:1], (mb, 128))
    c1 = jnp.broadcast_to(snap[:, 1:2], (mb, 128))

    def emit(q, first, count):
        def body(i, carry):
            at = pl.multiple_of(q * quarter + first + i * kc, kc)
            high, low = split(stack_ref[:, pl.ds(at, kc)])
            both = jnp.concatenate([high, low], axis=0)
            done = jnp.dot(left, both, preferred_element_type=F32)
            done = done[:mb] + done[mb:]
            for t in range(kc // 128):
                r = first // 128 + i * (kc // 128) + t
                out_ref[:, pl.ds(pl.multiple_of(at + t * 128, 128), 128)] = (
                    done[:, t * 128 : (t + 1) * 128]
                    + c0 * sn_ref[q, 0, pl.ds(r, 1), :]
                    + c1 * sn_ref[q, 1, pl.ds(r, 1), :]
                )
            return carry

        lax.fori_loop(0, count // kc, body, 0)
        where = pl.ds(pl.multiple_of(q * quarter + first, kc), count)
        copy = pltpu.make_async_copy(
            out_ref.at[:, where], modes_ref.at[:, where], out_sem.at[len(stores)]
        )
        copy.start()
        stores.append(copy)

    stores = []
    for copy in mates + forward_b + [sn_mate]:
        copy.wait()
    sn_forward = []
    for copy, source, g in sn_copies:
        copy.wait()
        i = pairs + g - 1
        forward = remote(sn_ref.at[source], sn_ref.at[source], sn_send.at[i], sn_recv.at[i], space, mate)
        forward.start()
        sn_forward.append(forward)
    emit(2 * pair, 0, quarter)
    emit(2 * pair + 1, 0, quarter)
    for forward in sn_forward:
        forward.wait()
    size = (pairs - 1) ** 2
    before = []
    for n in range(0, len(stage2), size or 1):
        group = stage2[n : n + size]
        forwards = []
        for copy, i, source, where, _, _ in group:
            copy.wait()
            rows = stack_ref.at[rows_of(source), where]
            forward = remote(rows, rows, fa_send.at[i], fa_recv.at[i], space, mate)
            forward.start()
            forwards.append(forward)
        finish(before, emit, pairs, piece_cols)
        before = list(zip(forwards, group))
    finish(before, emit, pairs, piece_cols)
    for copy in stores:
        copy.wait()


def finish(before, emit, pairs, piece_cols):
    for forward, _ in before:
        forward.wait()
    for _, (_, _, _, _, group, part) in before[: pairs - 1]:
        first = part * piece_cols
        quarter = PIECES * piece_cols
        emit(2 * group + first // quarter, first % quarter, piece_cols)


def per_device(n_space, n_mode, velocity, basis, levels, profile_index, advect):
    components, cx, cz, ny = velocity.shape
    mb, cols = basis.shape
    quarter = cols // n_mode
    nxb, nzb, nb = cx // STRIDE, cz // STRIDE, ny // STRIDE
    pairs = n_mode // 2
    pieces = max(1, 2 * PIECES * (pairs - 1) ** 2)
    dma = pltpu.SemaphoreType.DMA
    modes, sigma = pl.pallas_call(
        functools.partial(kernel, n_space, n_mode),
        out_shape=(
            jax.ShapeDtypeStruct((mb, cols), F32),
            jax.ShapeDtypeStruct((1, MODES), F32),
        ),
        in_specs=[
            pl.BlockSpec(memory_space=pl.ANY),
            pl.BlockSpec(memory_space=pl.ANY),
            pl.BlockSpec(memory_space=pltpu.SMEM),
            pl.BlockSpec(memory_space=pltpu.VMEM),
            pl.BlockSpec(memory_space=pltpu.VMEM),
            pl.BlockSpec(memory_space=pltpu.VMEM),
        ],
        out_specs=(
            pl.BlockSpec(memory_space=pl.ANY),
            pl.BlockSpec(memory_space=pltpu.VMEM),
        ),
        scratch_shapes=[
            pltpu.VMEM((mb, cols), F32),
            pltpu.VMEM((components, cx, cz + 16, ny), F32),
            pltpu.VMEM((n_mode * mb, cols), F32),
            pltpu.VMEM((6 * ny, 2 * nb), BF16),
            pltpu.VMEM((6 * ny, 2 * nb), BF16),
            pltpu.VMEM((2 * cz + 32, 6 * ny), BF16),
            pltpu.VMEM((nxb + 2, components, nzb, 2 * nb), F32),
            pltpu.VMEM((2, components, nzb, 2 * nb), F32),
            pltpu.VMEM((2, components * cx * 2, ny), F32),
            pltpu.VMEM((2, components * cx * 2, ny), F32),
            pltpu.VMEM((n_mode, 2, components * nxb * nzb // 2, 2 * nb), F32),
            pltpu.VMEM((16, quarter), F32),
            pltpu.VMEM((n_mode, 8 + n_mode * mb, 128), F32),
            pltpu.VMEM((n_space, 8 + n_mode * mb, 128), F32),
            dma((components,)), dma, dma((2 + 2 * PIECES * (pairs - 1),)),
            dma((2, n_mode - 1)), dma((2, n_mode - 1)),
            dma((pairs,)), dma((pairs,)),
            dma((pieces,)), dma((pieces,)),
            dma((max(1, pairs - 1),)), dma((max(1, pairs - 1),)),
            dma((pieces,)), dma((pieces,)),
            dma((2,)), dma((2,)),
            dma((2,)), dma((2,)),
            dma((2 * pairs - 1,)), dma((2 * pairs - 1,)),
            dma((n_mode - 1,)), dma((n_mode - 1,)),
            dma((n_space - 1,)), dma((n_space - 1,)),
        ],
        compiler_params=pltpu.CompilerParams(
            collective_id=0, has_side_effects=True, vmem_limit_bytes=56 * 1024 * 1024
        ),
    )(
        velocity,
        basis,
        levels,
        profile_index.reshape(1, -1),
        advect.reshape(1, -1),
        jnp.asarray(z_table(cz), BF16),
    )
    modes, sigma = pl.pallas_call(
        hand_over,
        out_shape=(
            jax.ShapeDtypeStruct((mb, cols), F32),
            jax.ShapeDtypeStruct((1, MODES), F32),
        ),
        in_specs=[pl.BlockSpec(memory_space=pl.ANY), pl.BlockSpec(memory_space=pltpu.VMEM)],
        out_specs=(
            pl.BlockSpec(memory_space=pl.ANY),
            pl.BlockSpec(memory_space=pltpu.VMEM),
        ),
        scratch_shapes=[pltpu.VMEM((mb, cols), F32), dma((8,)), dma((8,))],
        compiler_params=pltpu.CompilerParams(vmem_limit_bytes=60 * 1024 * 1024),
    )(modes, sigma)
    return modes, sigma.reshape(-1)


def hand_over(modes_ref, sigma_ref, out_ref, sigma_out_ref, held_ref, in_sem, out_sem):
    width = modes_ref.shape[1] // 8
    loads, stores = [], []
    for i in range(8):
        part = (slice(None), pl.ds(i * width, width))
        loads.append(pltpu.make_async_copy(modes_ref.at[part], held_ref.at[part], in_sem.at[i]))
        stores.append(pltpu.make_async_copy(held_ref.at[part], out_ref.at[part], out_sem.at[i]))
        loads[i].start()
    sigma_out_ref[...] = sigma_ref[...]
    for load, store in zip(loads, stores):
        load.wait()
        store.start()
    for store in stores:
        store.wait()


def solution(mesh):
    n_space, n_mode = mesh.shape["space"], mesh.shape["mode"]
    return jax.shard_map(
        functools.partial(per_device, n_space, n_mode),
        mesh=mesh,
        in_specs=(P(None, "space", "mode", None), P("mode", "space"), P(), P(), P()),
        out_specs=(P("mode", "space"), P()),
        check_vma=False,
    )
```
